128 devices in a mesh: gx: 16 (over z_hi, y, core), ta: 8 (over z_lo, x).
Axes of the slice: x: 4, y: 4, z: 4 (z_hi: 2, z_lo: 2; z = z_hi * 2 + z_lo), core: 2. Of those that a mesh axis runs over, the one named last changes fastest.
Arguments:
- initial_state: float32 [128, 256, 128], P('gx'), may hold values from -10 to 10
- reaction: float32 [128, 256, 128], P('gx'), may hold values from 0.02 to 0.1
- source: float32 [128, 256, 128], P('gx'), may hold values from -4 to 4
Outputs:
- interval_ends: float32 [8, 128, 256, 128], P('ta', 'gx')
The draws below stay inside these ranges and needn't reach their ends.
All inputs are finite; a program needn't handle non-finite values.
Results may differ from the reference program's by a relative error of at most 0.00002.
Values sent between devices are 32-bit elements; how exact they have to be, the bound alone decides.
No kernel may reach another device: no remote copies, remote signals or barrier semaphores. Data moves between devices by JAX's collectives and lax.ppermute only.
A program may use at most 64 MiB of HBM per device.

```python
import math
import jax
import jax.numpy as jnp

CX = 8
NY = 256
NZ = 128
STEPS = 8
ITERS = 2
NX = 128
N_GX = 16
N_TA = 8


def smooth_profile(count):
    position = jnp.arange(count, dtype=jnp.float32)
    return jnp.sin(math.pi * (position + 1.0) / (count + 1.0))


def draw_initial_state(key, part):
    key = jax.random.fold_in(key, 11)
    rough_key, sign_key, size_key = jax.random.split(key, 3)
    slabs = NX // CX
    rough = jnp.clip(jax.random.normal(rough_key, (NX, NY, NZ), jnp.float32), -4.0, 4.0)
    signs = 2.0 * jax.random.randint(sign_key, (slabs,), 0, 2).astype(jnp.float32) - 1.0
    sizes = jax.random.uniform(size_key, (slabs,), jnp.float32, 3.0, 5.0)
    per_plane = jnp.repeat(signs * sizes, CX, total_repeat_length=NX)
    profile_y = smooth_profile(NY)
    profile_z = smooth_profile(NZ)
    field = rough + per_plane[:, None, None] * profile_y[None, :, None] * profile_z[None, None, :]
    return field.astype(jnp.float32)


def block_scale(own_key, extent, pieces, low, top_value):
    loudness = 1.0
    for axis_at, blocks in pieces:
        draws = jax.random.uniform(jax.random.fold_in(jax.random.fold_in(own_key, 6), axis_at), (blocks,), jnp.float32, low / len(pieces), top_value / len(pieces))
        loudness = loudness * jnp.repeat(jnp.exp(draws), extent[axis_at] // blocks).reshape((-1,) + (1,) * (len(extent) - 1 - axis_at))
    return loudness


def bell_draw(rng, extent, scale, most, pieces=(), held_as=jnp.bfloat16):
    values = scale * jax.random.normal(rng, extent, jnp.float32)
    if pieces:
        values = values * block_scale(rng, extent, pieces, -0.22, 0.18)
    return jnp.clip(values, -most, most).astype(held_as)


def setup_inputs(seed: int = 0) -> dict:
    key_of = jax.random.split(jax.random.key(seed), 4)
    return {
        "initial_state": draw_initial_state(jax.random.fold_in(key_of[3], 71), 0),
        "reaction": jnp.clip(jnp.exp(math.log(0.1) - 1.609438 * jax.random.uniform(key_of[1], (NX, NY, NZ), jnp.float32) ** block_scale(key_of[1], (NX, NY, NZ), ((0, 16),), -0.2, 0.2)), 0.02, 0.1),
        "source": bell_draw(key_of[2], (NX, NY, NZ), 0.5, 4.0, ((0, 16),), jnp.float32),
    }


robin_weight = 0.5
diffusion = 0.1
speed_x = 0.2
speed_y = 0.1
speed_z = 0.1


def advance_field(field, lower_ghost, upper_ghost, reaction, source):
    stacked = jnp.concatenate([lower_ghost[:, None], field, upper_ghost[:, None]], axis=1)
    padded = jnp.pad(stacked, ((0, 0), (0, 0), (1, 1), (1, 1)))
    x_below = padded[:, :-2, 1:-1, 1:-1]
    x_above = padded[:, 2:, 1:-1, 1:-1]
    y_below = padded[:, 1:-1, :-2, 1:-1]
    y_above = padded[:, 1:-1, 2:, 1:-1]
    z_below = padded[:, 1:-1, 1:-1, :-2]
    z_above = padded[:, 1:-1, 1:-1, 2:]
    laplace = x_below + x_above + y_below + y_above + z_below + z_above - 6.0 * field
    advect = speed_x * (field - x_below) + speed_y * (field - y_below) + speed_z * (field - z_below)
    return (field + diffusion * laplace - advect + source) / (1.0 + reaction)


def run_interval(field, lower_series, upper_series, reaction, source, slabs):
    index = jnp.arange(slabs)[:, None, None]
    downs = []
    ups = []
    for moment in range(STEPS):
        first_plane = field[:, 0]
        second_plane = field[:, 1]
        last_plane = field[:, -1]
        before_last = field[:, -2]
        downs.append((second_plane - first_plane) + robin_weight * (first_plane + second_plane) / 2.0)
        ups.append((before_last - last_plane) + robin_weight * (last_plane + before_last) / 2.0)
        lower_ghost = (lower_series[moment] + (1.0 - robin_weight / 2.0) * first_plane) / (1.0 + robin_weight / 2.0)
        upper_ghost = (upper_series[moment] + (1.0 - robin_weight / 2.0) * last_plane) / (1.0 + robin_weight / 2.0)
        lower_ghost = jnp.where(index == 0, 0.0, lower_ghost)
        upper_ghost = jnp.where(index == slabs - 1, 0.0, upper_ghost)
        field = advance_field(field, lower_ghost, upper_ghost, reaction, source)
    return field, jnp.stack(downs), jnp.stack(ups)


def reference(initial_state, reaction, source):
    slabs = N_GX
    shape = (slabs, CX, NY, NZ)
    start = initial_state.reshape(shape)
    rates = reaction.reshape(shape)
    sources = source.reshape(shape)
    zero_series = jnp.zeros((STEPS, slabs, NY, NZ), jnp.float32)
    starts = [start for level in range(ITERS)]
    results = []
    for interval in range(N_TA):
        lower_series = zero_series
        upper_series = zero_series
        final_state = start
        for level in range(ITERS):
            final_state, downs, ups = run_interval(starts[level], lower_series, upper_series, rates, sources, slabs)
            starts[level] = final_state
            lower_series = jnp.concatenate([zero_series[:, :1], ups[:, :-1]], axis=1)
            upper_series = jnp.concatenate([downs[:, 1:], zero_series[:, :1]], axis=1)
        results.append(final_state.reshape((NX, NY, NZ)))
    return jnp.stack(results)
```

```python
import functools

import jax
import jax.numpy as jnp
from jax import lax
from jax.experimental import pallas as pl
from jax.experimental.pallas import tpu as pltpu
from jax.sharding import PartitionSpec as P

CX = 8
NZ = 128
STRIP = 32
HALO = 32
WINDOW = STRIP + 2 * HALO
WIDE = STRIP + 4 * HALO
PHASE = 32
STEPS = 8
PAD = 8
GROUP = 4
BY_MATRIX = 4

VMEM = pl.BlockSpec(memory_space=pltpu.VMEM)
SMEM = pl.BlockSpec(memory_space=pltpu.SMEM)
HBM = pl.BlockSpec(memory_space=pl.ANY)
PARAMS = pltpu.CompilerParams(vmem_limit_bytes=48 << 20)


def z_matrix():
    row = lax.broadcasted_iota(jnp.int32, (2 * NZ, NZ), 0) % NZ
    col = lax.broadcasted_iota(jnp.int32, (2 * NZ, NZ), 1)
    taps = jnp.where(row == col - 1, 2.0, 0.0) + jnp.where(row == col + 1, 1.0, 0.0)
    return taps.astype(jnp.bfloat16)


def z_sum(planes, taps):
    high = planes.astype(jnp.bfloat16)
    low = (planes - high.astype(jnp.float32)).astype(jnp.bfloat16)
    return jnp.dot(jnp.concatenate([high, low], 1), taps, preferred_element_type=jnp.float32)


def advance(src, dst, m, q, ghosts, edge, tiles, taps):
    lane = lax.broadcasted_iota(jnp.int32, (8, NZ), 1)
    not_first, not_last = lane != 0, lane != NZ - 1
    tiles = list(tiles)
    for begin in range(0, len(tiles), GROUP):
        group = tiles[begin : begin + GROUP]
        cells = [[src[x, PAD + 8 * t : PAD + 8 * t + 8, :] for x in range(CX)] for t in group]
        z_all = z_sum(jnp.concatenate([c[x] for c in cells for x in range(BY_MATRIX)], 0), taps)
        for at, t in enumerate(group):
            c = cells[at]
            low, high = ghosts(t)
            low = edge[0] * c[0] if low is None else edge[0] * c[0] + low
            high = edge[1] * c[-1] if high is None else edge[1] * c[-1] + high
            below = [low] + c[:-1]
            above = c[1:] + [high]
            for x in range(CX):
                y_below = src[x, PAD + 8 * t - 1 : PAD + 8 * t + 7, :]
                y_above = src[x, PAD + 8 * t + 1 : PAD + 8 * t + 9, :]
                if x < BY_MATRIX:
                    row = (at * BY_MATRIX + x) * 8
                    twice = below[x] + y_below
                    total = (twice + twice) + ((below[x] + above[x]) + y_above) + z_all[row : row + 8]
                else:
                    z_below = jnp.where(not_first, pltpu.roll(c[x], 1, 1), 0.0)
                    z_above = jnp.where(not_last, pltpu.roll(c[x], NZ - 1, 1), 0.0)
                    twice = below[x] + y_below + z_below
                    total = (twice + twice) + ((below[x] + above[x]) + (y_above + z_above))
                rows = slice(8 * t, 8 * t + 8)
                dst[x, PAD + 8 * t : PAD + 8 * t + 8, :] = total * m[x, rows, :] + q[x, rows, :]


def clear_pads(buffers, rows):
    for b in buffers:
        b[:, :PAD, :] = jnp.zeros((CX, PAD, NZ), jnp.float32)
        b[:, PAD + rows :, :] = jnp.zeros((CX, PAD, NZ), jnp.float32)


def no_ghosts(t):
    return None, None


def trace(src, place, t):
    rows = slice(PAD + 8 * t, PAD + 8 * t + 8)
    return src[place[2], rows, :] - 0.6 * src[place[1], rows, :]


def window_copies(arrays, bufs, sems, strip, blocks, start):
    for b in range(blocks):
        at = strip + start + b
        inside = jnp.logical_and(at >= 0, at < 8)
        row = pl.multiple_of(jnp.clip(at, 0, 7) * STRIP, STRIP)
        copies = [
            pltpu.make_async_copy(a.at[:, pl.ds(row, STRIP), :], v.at[:, pl.ds(b * STRIP, STRIP), :], sems.at[n, b])
            for n, (a, v) in enumerate(zip(arrays, bufs))
        ]
        yield b, inside, copies


def load_window(arrays, bufs, sems, strip, blocks, start, u_out, m_out, q_out, u_pad):
    for b, inside, copies in window_copies(arrays, bufs, sems, strip, blocks, start):
        for copy in copies:
            copy.start()
    for b, inside, copies in window_copies(arrays, bufs, sems, strip, blocks, start):
        for copy in copies:
            copy.wait()
        keep = jnp.where(inside, 1.0, 0.0)
        rows = slice(b * STRIP, (b + 1) * STRIP)
        scale = keep / (1.0 + bufs[1][:, rows, :])
        m_out[:, rows, :] = 0.1 * scale
        q_out[:, rows, :] = bufs[2][:, rows, :] * scale
        u_out[:, u_pad + b * STRIP : u_pad + (b + 1) * STRIP, :] = bufs[0][:, rows, :] * keep


def pack_kernel(place, u, r, s, out, ubuf, rbuf, sbuf, sems):
    load_window((u, r, s), (ubuf, rbuf, sbuf), sems, place[0], 3, -1, out.at[0], out.at[1], out.at[2], 0)


def first_a_kernel(place, edge, taps, u, r, s, trace_out, last, ubuf, rbuf, sbuf, ua, ub, m, q, sems):
    load_window((u, r, s), (ubuf, rbuf, sbuf), sems, place[0], 5, -2, ua, m, q, PAD)
    clear_pads((ua, ub), WIDE)
    edges = (edge[0], edge[1])
    t_matrix = taps[...]
    for k in range(PHASE // STEPS):
        def pair(p, _):
            for n, (src, dst) in enumerate(((ua, ub), (ub, ua))):
                step = k * STEPS + 2 * p + n
                for t in range(4 + k, 16 - k):
                    trace_out[step, 8 * (t - 4) : 8 * (t - 4) + 8, :] = trace(src, place, t)
                advance(src, dst, m, q, no_ghosts, edges, range(k, 20 - k), t_matrix)
            return 0
        lax.fori_loop(0, STEPS // 2, pair, 0)
    last[...] = ua[:, PAD + HALO : PAD + HALO + WINDOW, :]


def first_b_kernel(place, edge, taps, u, mine, trace_out, ua, ub):
    clear_pads((ua, ub), WINDOW)
    ua[:, PAD : PAD + WINDOW, :] = u[...]
    edges = (edge[0], edge[1])
    t_matrix = taps[...]
    for k in range(PHASE // STEPS):
        def pair(p, _):
            for n, (src, dst) in enumerate(((ua, ub), (ub, ua))):
                step = k * STEPS + 2 * p + n
                for t in range(k, 12 - k):
                    trace_out[step, 8 * t : 8 * t + 8, :] = trace(src, place, t)
                advance(src, dst, mine.at[1], mine.at[2], no_ghosts, edges, range(k, 12 - k), t_matrix)
            return 0
        lax.fori_loop(0, STEPS // 2, pair, 0)


def two_slabs(place, edge, taps, mine, other, series, ends, ua, ub, va, vb):
    odd = place[3] == 1
    own_edges = (edge[0], edge[1])
    other_edges = (edge[2], edge[3])
    t_matrix = taps[...]
    for k in range(PHASE // STEPS):
        def pair(p, _):
            for src, dst, osrc, odst, n in ((ua, ub, va, vb, 0), (ub, ua, vb, va, 1)):
                step = k * STEPS + 2 * p + n
                tiles = range(k, 12 - k)

                def ghosts(t):
                    far = trace(osrc, place, t)
                    near = series[step, 8 * t : 8 * t + 8, :]
                    return jnp.where(odd, near, far), jnp.where(odd, far, near)

                advance(src, dst, mine.at[1], mine.at[2], ghosts, own_edges, tiles, t_matrix)
                advance(osrc, odst, other.at[1], other.at[2], no_ghosts, other_edges, tiles, t_matrix)
            return 0
        lax.fori_loop(0, STEPS // 2, pair, 0)
        ends[k] = ua[:, PAD + HALO : PAD + HALO + STRIP, :]


def second_a_kernel(place, edge, taps, mine, other, series, ends, last, ua, ub, va, vb):
    clear_pads((ua, ub, va, vb), WINDOW)
    ua[:, PAD : PAD + WINDOW, :] = mine[0]
    va[:, PAD : PAD + WINDOW, :] = other[0]
    two_slabs(place, edge, taps, mine, other, series, ends, ua, ub, va, vb)
    last[0] = ua[:, PAD + HALO : PAD + HALO + STRIP, :]
    last[1] = va[:, PAD + HALO : PAD + HALO + STRIP, :]


def second_b_kernel(place, edge, taps, mine, other, series, left, mid, right, ends, ua, ub, va, vb):
    clear_pads((ua, ub, va, vb), WINDOW)
    for at, part in enumerate((left, mid, right)):
        rows = slice(PAD + at * STRIP, PAD + (at + 1) * STRIP)
        ua[:, rows, :] = part[0]
        va[:, rows, :] = part[1]
    two_slabs(place, edge, taps, mine, other, series, ends, ua, ub, va, vb)


def f32(*shape):
    return jax.ShapeDtypeStruct(shape, jnp.float32)


def buffer(rows):
    return pltpu.VMEM((CX, rows, NZ), jnp.float32)


def local(u, r, s):
    strip = lax.axis_index("ta")
    slab = lax.axis_index("gx")
    slabs = lax.axis_size("gx")
    strips = lax.axis_size("ta")
    odd = slab % 2
    other = slab - 1 + 2 * odd
    place = jnp.stack([strip, 7 - 7 * odd, 6 - 5 * odd, odd]).astype(jnp.int32)

    def weight(inside):
        return jnp.where(inside, 0.6, 0.0).astype(jnp.float32)

    edge = jnp.stack([weight(slab > 0), weight(slab < slabs - 1), weight(other > 0), weight(other < slabs - 1)])
    taps = z_matrix()

    mine = pl.pallas_call(
        pack_kernel,
        out_shape=f32(3, CX, WINDOW, NZ),
        in_specs=[SMEM, HBM, HBM, HBM],
        out_specs=VMEM,
        scratch_shapes=[buffer(WINDOW)] * 3 + [pltpu.SemaphoreType.DMA((3, 3))],
        compiler_params=PARAMS,
        name="pack_window",
    )(place, u, r, s)
    inter = [(i, i + 1) for i in range(1, slabs - 1, 2)]
    theirs = lax.ppermute(mine, "gx", inter + [(b, a) for a, b in inter])

    series_a, state = pl.pallas_call(
        first_a_kernel,
        out_shape=(f32(PHASE, WINDOW, NZ), f32(CX, WINDOW, NZ)),
        in_specs=[SMEM, SMEM, VMEM, HBM, HBM, HBM],
        out_specs=(VMEM, VMEM),
        scratch_shapes=[buffer(WIDE)] * 3 + [buffer(WIDE + 2 * PAD)] * 2 + [buffer(WIDE)] * 2 + [pltpu.SemaphoreType.DMA((3, 5))],
        compiler_params=PARAMS,
        name="first_iteration_a",
    )(place, edge, taps, u, r, s)
    intra = [(i, i + 1) for i in range(0, slabs, 2)]
    intra = intra + [(b, a) for a, b in intra]
    series_a = lax.ppermute(series_a, "gx", intra)
    series_b = pl.pallas_call(
        first_b_kernel,
        out_shape=f32(PHASE, WINDOW, NZ),
        in_specs=[SMEM, SMEM, VMEM, VMEM, VMEM],
        out_specs=VMEM,
        scratch_shapes=[buffer(WINDOW + 2 * PAD)] * 2,
        compiler_params=PARAMS,
        name="first_iteration_b",
    )(place, edge, taps, state, mine)
    series_b = lax.ppermute(series_b, "gx", intra)

    work = [buffer(WINDOW + 2 * PAD)] * 4
    ends_a, last = pl.pallas_call(
        second_a_kernel,
        out_shape=(f32(4, CX, STRIP, NZ), f32(2, CX, STRIP, NZ)),
        in_specs=[SMEM, SMEM] + [VMEM] * 4,
        out_specs=(VMEM, VMEM),
        scratch_shapes=work,
        compiler_params=PARAMS,
        name="second_iteration_a",
    )(place, edge, taps, mine, theirs, series_a)
    left = lax.ppermute(last, "ta", [(i, i + 1) for i in range(strips - 1)])
    right = lax.ppermute(last, "ta", [(i + 1, i) for i in range(strips - 1)])
    ends_b = pl.pallas_call(
        second_b_kernel,
        out_shape=f32(4, CX, STRIP, NZ),
        in_specs=[SMEM, SMEM] + [VMEM] * 7,
        out_specs=VMEM,
        scratch_shapes=work,
        compiler_params=PARAMS,
        name="second_iteration_b",
    )(place, edge, taps, mine, theirs, series_b, left, last, right)
    ends = jnp.concatenate([ends_a, ends_b], 0)
    return lax.all_to_all(ends, "ta", 0, 2, tiled=True)


def solution(mesh):
    return jax.shard_map(
        local,
        mesh=mesh,
        in_specs=(P("gx", None, None), P("gx", None, None), P("gx", None, None)),
        out_specs=P("ta", "gx", None, None),
        check_vma=False,
    )
```

```python
import jax
import jax.numpy as jnp
from jax import lax
from jax.experimental import pallas as pl
from jax.experimental.pallas import tpu as pltpu
from jax.sharding import PartitionSpec as P

CX = 8
NZ = 128
STRIP = 32
HALO = 32
WINDOW = STRIP + 2 * HALO
WIDE = STRIP + 4 * HALO
PHASE = 32
STEPS = 8
PAD = 8
SERIES = STEPS * sum(range(WINDOW, STRIP, -16))
GROUP = 4
SNAKE = (0, 1, 2, 3, 7, 6, 5, 4)
BY_MATRIX = 4

VMEM = pl.BlockSpec(memory_space=pltpu.VMEM)
HBM = pl.BlockSpec(memory_space=pltpu.HBM)
ANY = pl.BlockSpec(memory_space=pl.ANY)


def z_matrix(taps):
    row = lax.broadcasted_iota(jnp.int32, (NZ, NZ), 0)
    col = lax.broadcasted_iota(jnp.int32, (NZ, NZ), 1)
    half = jnp.where(row == col - 1, 2.0, 0.0) + jnp.where(row == col + 1, 1.0, 0.0)
    taps[:NZ, :] = half.astype(jnp.bfloat16)
    taps[NZ:, :] = half.astype(jnp.bfloat16)
    return taps[...]


def position():
    interval = lax.axis_index("ta")
    slab = lax.axis_index("gx")
    slabs = lax.axis_size("gx")
    strip = jnp.where(interval < 4, interval, 11 - interval)
    odd = lax.rem(slab, 2) == 1

    def edges(at):
        return jnp.where(at > 0, 0.6, 0.0), jnp.where(at < slabs - 1, 0.6, 0.0)

    return strip, odd, edges(slab), edges(jnp.where(odd, slab + 1, slab - 1))


def z_sum(planes, taps):
    high = planes.astype(jnp.bfloat16)
    low = (planes - high.astype(jnp.float32)).astype(jnp.bfloat16)
    return jnp.dot(jnp.concatenate([high, low], 1), taps, preferred_element_type=jnp.float32)


def advance(src, dst, m, q, ghosts, edge, tiles, taps):
    lane = lax.broadcasted_iota(jnp.int32, (8, NZ), 1)
    not_first, not_last = lane != 0, lane != NZ - 1
    tiles = list(tiles)
    for begin in range(0, len(tiles), GROUP):
        group = tiles[begin : begin + GROUP]
        cells = [[src[x, PAD + 8 * t : PAD + 8 * t + 8, :] for x in range(CX)] for t in group]
        z_all = z_sum(jnp.concatenate([c[x] for c in cells for x in range(BY_MATRIX)], 0), taps)
        for at, t in enumerate(group):
            c = cells[at]
            low, high = ghosts(t, c)
            low = edge[0] * c[0] if low is None else edge[0] * c[0] + low
            high = edge[1] * c[-1] if high is None else edge[1] * c[-1] + high
            below = [low] + c[:-1]
            above = c[1:] + [high]
            for x in range(CX):
                y_below = src[x, PAD + 8 * t - 1 : PAD + 8 * t + 7, :]
                y_above = src[x, PAD + 8 * t + 1 : PAD + 8 * t + 9, :]
                if x < BY_MATRIX:
                    row = (at * BY_MATRIX + x) * 8
                    twice = below[x] + y_below
                    total = (twice + twice) + ((below[x] + above[x]) + y_above) + z_all[row : row + 8]
                else:
                    z_below = jnp.where(not_first, pltpu.roll(c[x], 1, 1), 0.0)
                    z_above = jnp.where(not_last, pltpu.roll(c[x], NZ - 1, 1), 0.0)
                    twice = below[x] + y_below + z_below
                    total = (twice + twice) + ((below[x] + above[x]) + (y_above + z_above))
                rows = slice(8 * t, 8 * t + 8)
                dst[x, PAD + 8 * t : PAD + 8 * t + 8, :] = total * m[x, rows, :] + q[x, rows, :]


def clear_pads(buffers, rows):
    for b in buffers:
        b[:, :PAD, :] = jnp.zeros((CX, PAD, NZ), jnp.float32)
        b[:, PAD + rows :, :] = jnp.zeros((CX, PAD, NZ), jnp.float32)


def traces(c):
    return c[CX - 2] - 0.6 * c[CX - 1], c[1] - 0.6 * c[0]


def series_rows(k, step, t):
    base = STEPS * sum(WINDOW - 16 * before for before in range(k))
    return pl.ds(pl.multiple_of(base + step * (WINDOW - 16 * k) + 8 * (t - k), 8), 8)


def window_blocks(strip, blocks, start):
    for b in range(blocks):
        at = strip + start + b
        inside = jnp.logical_and(at >= 0, at < 8)
        yield b, pl.multiple_of(jnp.clip(at, 0, 7) * STRIP, STRIP), jnp.where(inside, 1.0, 0.0)


def pack_kernel(u, r, s, out, ubuf, rbuf, sbuf, sems):
    strip, _, _, _ = position()
    copies = []
    for b, row, keep in window_blocks(strip, 3, -1):
        rows = pl.ds(b * STRIP, STRIP)
        for n, (a, v) in enumerate(((u, ubuf), (r, rbuf), (s, sbuf))):
            copies.append(pltpu.make_async_copy(a.at[:, pl.ds(row, STRIP), :], v.at[:, rows, :], sems.at[n, b]))
    for copy in copies:
        copy.start()
    for b, row, keep in window_blocks(strip, 3, -1):
        for copy in copies[3 * b : 3 * b + 3]:
            copy.wait()
        rows = slice(b * STRIP, (b + 1) * STRIP)
        scale = keep / (1.0 + rbuf[:, rows, :])
        out[0, :, rows, :] = ubuf[:, rows, :] * keep
        out[1, :, rows, :] = 0.1 * scale
        out[2, :, rows, :] = sbuf[:, rows, :] * scale


def phase(body):
    for k in range(PHASE // STEPS):
        def pair(p, _):
            for n in range(2):
                body(k, 2 * p + n, n)
            return 0
        lax.fori_loop(0, STEPS // 2, pair, 0)
        yield k


def first_a_kernel(u, r, s, packed, near_out, last, taps, ua, ub, m, q):
    strip, odd, edges, _ = position()
    for b, row, keep in window_blocks(strip, 5, -2):
        rows = slice(b * STRIP, (b + 1) * STRIP)
        scale = keep / (1.0 + r[:, pl.ds(row, STRIP), :])
        m[:, rows, :] = 0.1 * scale
        q[:, rows, :] = s[:, pl.ds(row, STRIP), :] * scale
        ua[:, PAD + b * STRIP : PAD + (b + 1) * STRIP, :] = u[:, pl.ds(row, STRIP), :] * keep
    clear_pads((ua, ub), WIDE)
    t_matrix = z_matrix(taps)

    def step(k, at, n):
        def ghosts(t, c):
            if 4 + k <= t < 16 - k:
                up, down = traces(c)
                near_out[series_rows(k, at, t - 4), :] = jnp.where(odd, down, up)
            return None, None

        src, dst = ((ua, ub), (ub, ua))[n]
        advance(src, dst, m, q, ghosts, edges, range(k, 20 - k), t_matrix)

    for _ in phase(step):
        pass
    last[...] = ua[:, PAD + HALO : PAD + HALO + WINDOW, :]


def first_b_kernel(u, mine, near_out, far_out, taps, ua, ub):
    _, odd, edges, _ = position()
    clear_pads((ua, ub), WINDOW)
    ua[:, PAD : PAD + WINDOW, :] = u[...]
    t_matrix = z_matrix(taps)

    def step(k, at, n):
        def ghosts(t, c):
            up, down = traces(c)
            rows = series_rows(k, at, t)
            near_out[rows, :] = jnp.where(odd, down, up)
            far_out[rows, :] = jnp.where(odd, up, down)
            return None, None

        src, dst = ((ua, ub), (ub, ua))[n]
        advance(src, dst, mine.at[1], mine.at[2], ghosts, edges, range(k, 12 - k), t_matrix)

    for _ in phase(step):
        pass


def second_a_kernel(mine, other, near_series, ends, taps, ua, ub, va, vb):
    _, odd, own_edges, other_edges = position()
    clear_pads((ua, ub, va, vb), WINDOW)
    ua[:, PAD : PAD + WINDOW, :] = mine[0]
    va[:, PAD : PAD + WINDOW, :] = other[0]
    t_matrix = z_matrix(taps)

    def step(k, at, n):
        src, dst, osrc, odst = ((ua, ub, va, vb), (ub, ua, vb, va))[n]

        def ghosts(t, c):
            rows = slice(PAD + 8 * t, PAD + 8 * t + 8)
            up, down = traces({x: osrc[x, rows, :] for x in (0, 1, CX - 2, CX - 1)})
            near = near_series[series_rows(k, at, t), :]
            return jnp.where(odd, near, up), jnp.where(odd, down, near)

        tiles = range(k, 12 - k)
        advance(src, dst, mine.at[1], mine.at[2], ghosts, own_edges, tiles, t_matrix)
        advance(osrc, odst, other.at[1], other.at[2], lambda t, c: (None, None), other_edges, tiles, t_matrix)

    for k in phase(step):
        ends[k] = ua[:, PAD + HALO : PAD + HALO + STRIP, :]


def second_b_kernel(mine, near_series, far_series, even_swap, mid, odd_swap, ends, taps, ua, ub):
    strip, odd, edges, _ = position()
    clear_pads((ua, ub), WINDOW)
    odd_strip = lax.rem(strip, 2) == 1

    def put(left, right):
        for at, part in enumerate((left, mid, right)):
            ua[:, PAD + at * STRIP : PAD + (at + 1) * STRIP, :] = part[...]

    pl.when(odd_strip)(lambda: put(even_swap, odd_swap))
    pl.when(jnp.logical_not(odd_strip))(lambda: put(odd_swap, even_swap))
    t_matrix = z_matrix(taps)

    def step(k, at, n):
        def ghosts(t, c):
            rows = series_rows(k, at, t)
            near, far = near_series[rows, :], far_series[rows, :]
            return jnp.where(odd, near, far), jnp.where(odd, far, near)

        src, dst = ((ua, ub), (ub, ua))[n]
        advance(src, dst, mine.at[1], mine.at[2], ghosts, edges, range(k, 12 - k), t_matrix)

    for k in phase(step):
        ends[k] = ua[:, PAD + HALO : PAD + HALO + STRIP, :]


def swaps(some, others):
    pairs = list(zip(some, others))
    return pairs + [(b, a) for a, b in pairs]


def f32(*shape):
    return jax.ShapeDtypeStruct(shape, jnp.float32)


def buffer(rows):
    return pltpu.VMEM((CX, rows, NZ), jnp.float32)


def local(u, r, s):
    slabs = lax.axis_size("gx")

    def kernel(body, outs, ins, scratch, name, micros, vmem=48):
        return pl.pallas_call(
            body,
            out_shape=outs,
            in_specs=ins,
            out_specs=jax.tree.map(lambda _: VMEM, outs),
            scratch_shapes=scratch,
            compiler_params=pltpu.CompilerParams(vmem_limit_bytes=vmem << 20),
            cost_estimate=pl.CostEstimate(flops=0, transcendentals=0, bytes_accessed=int(micros * 3.6e6)),
            name=name,
        )

    taps = pltpu.VMEM((2 * NZ, NZ), jnp.bfloat16)
    padded = buffer(WINDOW + 2 * PAD)
    mine = kernel(
        pack_kernel, f32(3, CX, WINDOW, NZ), [HBM, HBM, HBM],
        [buffer(WINDOW)] * 3 + [pltpu.SemaphoreType.DMA((3, 3))], "pack_window", 2.0, 62,
    )(u, r, s)
    far_swap = swaps(range(1, slabs - 1, 2), range(2, slabs, 2))
    near_swap = swaps(range(0, slabs, 2), range(1, slabs, 2))
    theirs = lax.ppermute(mine, "gx", far_swap)

    series = f32(SERIES, NZ)
    near_a, state = kernel(
        first_a_kernel, (series, f32(CX, WINDOW, NZ)), [VMEM, VMEM, VMEM, ANY],
        [taps] + [buffer(WIDE + 2 * PAD)] * 2 + [buffer(WIDE)] * 2,
        "first_iteration_a", 11.0,
    )(u, r, s, mine)
    near_a = lax.ppermute(near_a, "gx", near_swap)
    near_b, far_b = kernel(
        first_b_kernel, (series, series), [VMEM, VMEM], [taps] + [padded] * 2, "first_iteration_b", 6.0
    )(state, mine)
    near_b = lax.ppermute(near_b, "gx", near_swap)
    far_b = lax.ppermute(far_b, "gx", far_swap)

    ends_a = kernel(
        second_a_kernel, f32(4, CX, STRIP, NZ), [VMEM] * 3, [taps] + [padded] * 4, "second_iteration_a", 12.0
    )(mine, theirs, near_a)
    last = ends_a[3]
    even_swap = lax.ppermute(last, "ta", swaps(SNAKE[0::2], SNAKE[1::2]))
    odd_swap = lax.ppermute(last, "ta", swaps(SNAKE[1:-1:2], SNAKE[2::2]))
    ends_b = kernel(
        second_b_kernel, f32(4, CX, STRIP, NZ), [VMEM] * 6, [taps] + [padded] * 2, "second_iteration_b", 7.0
    )(mine, near_b, far_b, even_swap, last, odd_swap)
    ends = jnp.concatenate([ends_a, ends_b], 0)
    strips = lax.all_to_all(ends, "ta", 0, 0, tiled=True)
    return jnp.concatenate([strips[i] for i in SNAKE], 1)[None]


def solution(mesh):
    return jax.shard_map(
        local,
        mesh=mesh,
        in_specs=(P("gx", None, None), P("gx", None, None), P("gx", None, None)),
        out_specs=P("ta", "gx", None, None),
        check_vma=False,
    )
```

```python
import jax
import jax.numpy as jnp
from jax import lax
from jax.experimental import pallas as pl
from jax.experimental.pallas import tpu as pltpu
from jax.sharding import PartitionSpec as P

CX = 8
NZ = 128
STRIP = 32
HALO = 32
WINDOW = STRIP + 2 * HALO
WIDE = STRIP + 4 * HALO
PHASE = 32
STEPS = 8
PAD = 8
MIDDLE = WIDE - 32
GROUP = 4
SNAKE = (0, 1, 2, 3, 7, 6, 5, 4)
BY_MATRIX = 4

VMEM = pl.BlockSpec(memory_space=pltpu.VMEM)
ANY = pl.BlockSpec(memory_space=pl.ANY)
HBM = pl.BlockSpec(memory_space=pltpu.HBM)


def z_matrix(taps):
    row = lax.broadcasted_iota(jnp.int32, (NZ, NZ), 0)
    col = lax.broadcasted_iota(jnp.int32, (NZ, NZ), 1)
    half = jnp.where(row == col - 1, 2.0, 0.0) + jnp.where(row == col + 1, 1.0, 0.0)
    taps[:NZ, :] = half.astype(jnp.bfloat16)
    taps[NZ:, :] = half.astype(jnp.bfloat16)
    return taps[...]


def position():
    interval = lax.axis_index("ta")
    slab = lax.axis_index("gx")
    slabs = lax.axis_size("gx")
    strip = jnp.where(interval < 4, interval, 11 - interval)
    edges = jnp.where(slab > 0, 0.6, 0.0), jnp.where(slab < slabs - 1, 0.6, 0.0)
    return strip, lax.rem(slab, 2) == 1, edges


def z_sum(planes, taps):
    high = planes.astype(jnp.bfloat16)
    low = (planes - high.astype(jnp.float32)).astype(jnp.bfloat16)
    return jnp.dot(jnp.concatenate([high, low], 1), taps, preferred_element_type=jnp.float32)


def advance(src, dst, m, q, ghosts, edge, tiles, taps):
    lane = lax.broadcasted_iota(jnp.int32, (8, NZ), 1)
    not_first, not_last = lane != 0, lane != NZ - 1
    tiles = list(tiles)
    for begin in range(0, len(tiles), GROUP):
        group = tiles[begin : begin + GROUP]
        cells = [[src[x, PAD + 8 * t : PAD + 8 * t + 8, :] for x in range(CX)] for t in group]
        z_all = z_sum(jnp.concatenate([c[x] for c in cells for x in range(BY_MATRIX)], 0), taps)
        for at, t in enumerate(group):
            c = cells[at]
            low, high = ghosts(t, c)
            low = edge[0] * c[0] if low is None else edge[0] * c[0] + low
            high = edge[1] * c[-1] if high is None else edge[1] * c[-1] + high
            below = [low] + c[:-1]
            above = c[1:] + [high]
            for x in range(CX):
                y_below = src[x, PAD + 8 * t - 1 : PAD + 8 * t + 7, :]
                y_above = src[x, PAD + 8 * t + 1 : PAD + 8 * t + 9, :]
                if x < BY_MATRIX:
                    row = (at * BY_MATRIX + x) * 8
                    twice = below[x] + y_below
                    total = (twice + twice) + ((below[x] + above[x]) + y_above) + z_all[row : row + 8]
                else:
                    z_below = jnp.where(not_first, pltpu.roll(c[x], 1, 1), 0.0)
                    z_above = jnp.where(not_last, pltpu.roll(c[x], NZ - 1, 1), 0.0)
                    twice = below[x] + y_below + z_below
                    total = (twice + twice) + ((below[x] + above[x]) + (y_above + z_above))
                rows = slice(8 * t, 8 * t + 8)
                dst[x, PAD + 8 * t : PAD + 8 * t + 8, :] = total * m[x, rows, :] + q[x, rows, :]


def clear_pads(buffers, rows):
    for b in buffers:
        b[:, :PAD, :] = jnp.zeros((CX, PAD, NZ), jnp.float32)
        b[:, PAD + rows :, :] = jnp.zeros((CX, PAD, NZ), jnp.float32)


def traces(c):
    return c[CX - 2] - 0.6 * c[CX - 1], c[1] - 0.6 * c[0]


def series_rows(k, step, t, first=0):
    base = STEPS * sum(WINDOW - 16 * before for before in range(first, k))
    return pl.ds(pl.multiple_of(base + step * (WINDOW - 16 * k) + 8 * (t - k), 8), 8)


def load_window(u, r, s, ubuf, rbuf, sbuf, sems, strip, height, put):
    halo = (height - STRIP) // 2
    first = strip * STRIP - halo
    start = pl.multiple_of(jnp.clip(first, 0, u.shape[1] - height), STRIP)
    landing = pl.multiple_of(halo + start - first, STRIP)
    copies = [
        pltpu.make_async_copy(a.at[:, pl.ds(start, height), :], v.at[:, pl.ds(landing, height), :], sems.at[n])
        for n, (a, v) in enumerate(((u, ubuf), (r, rbuf), (s, sbuf)))
    ]
    for copy in copies:
        copy.start()
    for copy in copies:
        copy.wait()
    for b in range(height // STRIP):
        at = strip + b - halo // STRIP
        keep = jnp.logical_and(at >= 0, at < u.shape[1] // STRIP)
        here = slice(halo + b * STRIP, halo + (b + 1) * STRIP)
        scale = 1.0 / (1.0 + rbuf[:, here, :])
        parts = ubuf[:, here, :], 0.1 * scale, sbuf[:, here, :] * scale
        put(slice(b * STRIP, (b + 1) * STRIP), [jnp.where(keep, part, 0.0) for part in parts])


def phase(body, intervals=range(PHASE // STEPS)):
    for k in intervals:
        def pair(p, _):
            for n in range(2):
                body(k, 2 * p + n, n)
            return 0
        lax.fori_loop(0, STEPS // 2, pair, 0)
        yield k


def first_iteration(m, q, near_out, far_out, taps, ua, ub, odd, edges, intervals, margin):
    t_matrix = z_matrix(taps)
    begin = intervals[0]

    def step(k, at, n):
        def ghosts(t, c):
            t = t - margin
            if k <= t < WINDOW // 8 - k:
                up, down = traces(c)
                rows = series_rows(k, at, t, begin)
                near_out[rows, :] = jnp.where(odd, down, up)
                far_out[rows, :] = jnp.where(odd, up, down)
            return None, None

        src, dst = ((ua, ub), (ub, ua))[n]
        tiles = m.shape[1] // 8
        advance(src, dst, m, q, ghosts, edges, range(k - begin, tiles - k + begin), t_matrix)

    for _ in phase(step, intervals):
        pass


def first_a_kernel(u, r, s, near_out, far_out, kept, start, taps, ubuf, rbuf, sbuf, ua, ub, m, q, sems):
    strip, odd, edges = position()

    def put(rows, parts):
        ua[:, PAD + rows.start : PAD + rows.stop, :], m[:, rows, :], q[:, rows, :] = parts

    clear_pads((ua, ub), WIDE)
    load_window(u, r, s, ubuf, rbuf, sbuf, sems, strip, WIDE, put)
    start[...] = ua[:, PAD + HALO : PAD + HALO + WINDOW, :]
    first_iteration(m, q, near_out, far_out, taps, ua, ub, odd, edges, (0, 1), 4)
    kept[0] = ua[:, PAD + 16 : PAD + 16 + MIDDLE, :]
    kept[1] = m[:, 16 : 16 + MIDDLE, :]
    kept[2] = q[:, 16 : 16 + MIDDLE, :]


def first_b_kernel(kept, near_in, far_in, near_out, far_out, last, taps, ua, ub):
    _, odd, edges = position()
    clear_pads((ua, ub), MIDDLE)
    ua[:, PAD : PAD + MIDDLE, :] = kept[0]
    before = near_in.shape[0]
    near_out[:before, :] = near_in[...]
    far_out[:before, :] = far_in[...]
    rest = pl.ds(before, near_out.shape[0] - before)
    first_iteration(
        kept.at[1], kept.at[2], near_out.at[rest, :], far_out.at[rest, :], taps, ua, ub, odd, edges, (2, 3), 2
    )
    last[...] = ua[:, PAD + 16 : PAD + 16 + WINDOW, :]


def inner(kept):
    return [kept.at[n, :, pl.ds(16, WINDOW), :] for n in (1, 2)]


def first_c_kernel(u, kept, near_out, far_out, taps, ua, ub):
    _, odd, edges = position()
    clear_pads((ua, ub), WINDOW)
    ua[:, PAD : PAD + WINDOW, :] = u[...]
    first_iteration(*inner(kept), near_out, far_out, taps, ua, ub, odd, edges, range(4), 0)


def second_iteration(kept, near, far, ends, taps, ua, ub, odd, edges):
    t_matrix = z_matrix(taps)
    m, q = inner(kept)

    def step(k, at, n):
        def ghosts(t, c):
            rows = series_rows(k, at, t)
            near_trace, far_trace = near[rows, :], far[rows, :]
            return jnp.where(odd, near_trace, far_trace), jnp.where(odd, far_trace, near_trace)

        src, dst = ((ua, ub), (ub, ua))[n]
        advance(src, dst, m, q, ghosts, edges, range(k, WINDOW // 8 - k), t_matrix)

    for k in phase(step):
        ends[k] = ua[:, PAD + HALO : PAD + HALO + STRIP, :]


def second_a_kernel(start, kept, near, far, ends, taps, ua, ub):
    _, odd, edges = position()
    clear_pads((ua, ub), WINDOW)
    ua[:, PAD : PAD + WINDOW, :] = start[...]
    second_iteration(kept, near, far, ends, taps, ua, ub, odd, edges)


def second_b_kernel(kept, near, far, even_swap, mid, odd_swap, ends, taps, ua, ub):
    strip, odd, edges = position()
    clear_pads((ua, ub), WINDOW)
    odd_strip = lax.rem(strip, 2) == 1

    def put(left, right):
        for at, part in enumerate((left, mid, right)):
            ua[:, PAD + at * STRIP : PAD + (at + 1) * STRIP, :] = part[...]

    pl.when(odd_strip)(lambda: put(even_swap, odd_swap))
    pl.when(jnp.logical_not(odd_strip))(lambda: put(odd_swap, even_swap))
    second_iteration(kept, near, far, ends, taps, ua, ub, odd, edges)


def swaps(some, others):
    pairs = list(zip(some, others))
    return pairs + [(b, a) for a, b in pairs]


def buffer(rows):
    return pltpu.VMEM((CX, rows, NZ), jnp.float32)


def local(u, r, s):
    slabs = lax.axis_size("gx")
    taps = pltpu.VMEM((2 * NZ, NZ), jnp.bfloat16)
    padded = buffer(WINDOW + 2 * PAD)

    def out(*shape):
        return pltpu.VMEM(shape, jnp.float32)

    def kernel(body, outs, ins, scratch, name, micros, after=0):
        def run(*refs):
            body(*refs[: len(ins)], *refs[len(ins) + after :])

        return pl.pallas_call(
            run,
            out_shape=outs,
            in_specs=ins + [ANY] * after,
            out_specs=jax.tree.map(lambda _: VMEM, outs),
            scratch_shapes=scratch,
            compiler_params=pltpu.CompilerParams(vmem_limit_bytes=40 << 20),
            cost_estimate=pl.CostEstimate(flops=0, transcendentals=0, bytes_accessed=int(micros * 3.6e6)),
            name=name,
        )

    far_swap = swaps(range(1, slabs - 1, 2), range(2, slabs, 2))
    near_swap = swaps(range(0, slabs, 2), range(1, slabs, 2))
    early, late = (STEPS * (2 * WINDOW - 16 - 64 * n) for n in range(2))

    u, r, s = (pltpu.with_memory_space_constraint(a, pltpu.HBM) for a in (u, r, s))
    wide_work = [buffer(WIDE + 4 * HALO)] * 3 + [buffer(WIDE + 2 * PAD)] * 2 + [buffer(WIDE)] * 2
    near_a, far_a, kept, start = kernel(
        first_a_kernel,
        (out(early, NZ), out(early, NZ), out(3, CX, MIDDLE, NZ), out(CX, WINDOW, NZ)),
        [HBM] * 3, [taps] + wide_work + [pltpu.SemaphoreType.DMA((3,))], "first_iteration_a", 0.01,
    )(u, r, s)
    series = out(early + late, NZ)
    near_b, far_b, state = kernel(
        first_b_kernel, (series, series, out(CX, WINDOW, NZ)),
        [VMEM] * 3, [taps] + [buffer(MIDDLE + 2 * PAD)] * 2, "first_iteration_b", 3.0,
    )(kept, near_a, far_a)
    near_c, far_c = kernel(
        first_c_kernel, (series, series), [VMEM, VMEM], [taps] + [padded] * 2, "first_iteration_c", 3.0, 2
    )(state, kept, near_b, far_b)
    theirs = [
        (lax.ppermute(near, "gx", near_swap), lax.ppermute(far, "gx", far_swap))
        for near, far in ((near_b, far_b), (near_c, far_c))
    ]
    ends_a = kernel(
        second_a_kernel, out(4, CX, STRIP, NZ), [VMEM] * 4, [taps] + [padded] * 2, "second_iteration_a", 12.0, 2
    )(start, kept, *theirs[0], near_c, far_c)
    last = ends_a[3]
    even_swap = lax.ppermute(last, "ta", swaps(SNAKE[0::2], SNAKE[1::2]))
    odd_swap = lax.ppermute(last, "ta", swaps(SNAKE[1:-1:2], SNAKE[2::2]))
    ends_b = kernel(
        second_b_kernel, out(4, CX, STRIP, NZ), [VMEM] * 6, [taps] + [padded] * 2, "second_iteration_b", 3.0
    )(kept, *theirs[1], even_swap, last, odd_swap)
    ends = jnp.concatenate([ends_a, ends_b], 0)
    strips = lax.all_to_all(ends, "ta", 0, 0, tiled=True)
    return jnp.concatenate([strips[i] for i in SNAKE], 1)[None]


def solution(mesh):
    return jax.shard_map(
        local,
        mesh=mesh,
        in_specs=(P("gx", None, None), P("gx", None, None), P("gx", None, None)),
        out_specs=P("ta", "gx", None, None),
        check_vma=False,
    )
```

```python
import jax
import jax.numpy as jnp
from jax import lax
from jax.experimental import pallas as pl
from jax.experimental.pallas import tpu as pltpu
from jax.sharding import PartitionSpec as P

CX = 8
NZ = 128
STRIP = 32
HALO = 32
WINDOW = STRIP + 2 * HALO
PHASE = 32
STEPS = 8
PAD = 8
SERIES = STEPS * sum(range(WINDOW, STRIP, -16))
GROUP = 4
SNAKE = (0, 1, 2, 3, 7, 6, 5, 4)
BY_MATRIX = 4

VMEM = pl.BlockSpec(memory_space=pltpu.VMEM)
ANY = pl.BlockSpec(memory_space=pl.ANY)
HBM = pl.BlockSpec(memory_space=pltpu.HBM)


def z_matrix(taps):
    row = lax.broadcasted_iota(jnp.int32, (NZ, NZ), 0)
    col = lax.broadcasted_iota(jnp.int32, (NZ, NZ), 1)
    half = jnp.where(row == col - 1, 2.0, 0.0) + jnp.where(row == col + 1, 1.0, 0.0)
    taps[:NZ, :] = half.astype(jnp.bfloat16)
    taps[NZ:, :] = half.astype(jnp.bfloat16)
    return taps[...]


def position():
    interval = lax.axis_index("ta")
    slab = lax.axis_index("gx")
    slabs = lax.axis_size("gx")
    strip = jnp.where(interval < 4, interval, 11 - interval)
    strip = jnp.where(slab < slabs // 2, strip, 7 - strip)
    edges = jnp.where(slab > 0, 0.6, 0.0), jnp.where(slab < slabs - 1, 0.6, 0.0)
    return strip, lax.rem(slab, 2) == 1, edges


def z_sum(planes, taps):
    high = planes.astype(jnp.bfloat16)
    low = (planes - high.astype(jnp.float32)).astype(jnp.bfloat16)
    return jnp.dot(jnp.concatenate([high, low], 1), taps, preferred_element_type=jnp.float32)


def advance(src, dst, m, q, ghosts, edge, tiles, taps):
    lane = lax.broadcasted_iota(jnp.int32, (8, NZ), 1)
    not_first, not_last = lane != 0, lane != NZ - 1
    tiles = list(tiles)
    for begin in range(0, len(tiles), GROUP):
        group = tiles[begin : begin + GROUP]
        cells = [[src[x, PAD + 8 * t : PAD + 8 * t + 8, :] for x in range(CX)] for t in group]
        z_all = z_sum(jnp.concatenate([c[x] for c in cells for x in range(BY_MATRIX)], 0), taps)
        for at, t in enumerate(group):
            c = cells[at]
            low, high = ghosts(t, c)
            low = edge[0] * c[0] if low is None else edge[0] * c[0] + low
            high = edge[1] * c[-1] if high is None else edge[1] * c[-1] + high
            below = [low] + c[:-1]
            above = c[1:] + [high]
            for x in range(CX):
                y_below = src[x, PAD + 8 * t - 1 : PAD + 8 * t + 7, :]
                y_above = src[x, PAD + 8 * t + 1 : PAD + 8 * t + 9, :]
                if x < BY_MATRIX:
                    row = (at * BY_MATRIX + x) * 8
                    twice = below[x] + y_below
                    total = (twice + twice) + ((below[x] + above[x]) + y_above) + z_all[row : row + 8]
                else:
                    z_below = jnp.where(not_first, pltpu.roll(c[x], 1, 1), 0.0)
                    z_above = jnp.where(not_last, pltpu.roll(c[x], NZ - 1, 1), 0.0)
                    twice = below[x] + y_below + z_below
                    total = (twice + twice) + ((below[x] + above[x]) + (y_above + z_above))
                rows = slice(8 * t, 8 * t + 8)
                dst[x, PAD + 8 * t : PAD + 8 * t + 8, :] = total * m[x, rows, :] + q[x, rows, :]


def clear_pads(buffers, rows):
    for b in buffers:
        b[:, :PAD, :] = jnp.zeros((CX, PAD, NZ), jnp.float32)
        b[:, PAD + rows :, :] = jnp.zeros((CX, PAD, NZ), jnp.float32)


def traces(c):
    return c[CX - 2] - 0.6 * c[CX - 1], c[1] - 0.6 * c[0]


def series_rows(k, step, t):
    base = STEPS * sum(WINDOW - 16 * before for before in range(k))
    return pl.ds(pl.multiple_of(base + step * (WINDOW - 16 * k) + 8 * (t - k), 8), 8)


def load_window(u, r, s, ubuf, rbuf, sbuf, sems, strip, height, put):
    halo = (height - STRIP) // 2
    first = strip * STRIP - halo
    start = pl.multiple_of(jnp.clip(first, 0, u.shape[1] - height), STRIP)
    landing = pl.multiple_of(halo + start - first, STRIP)
    copies = [
        pltpu.make_async_copy(a.at[:, pl.ds(start, height), :], v.at[:, pl.ds(landing, height), :], sems.at[n])
        for n, (a, v) in enumerate(((u, ubuf), (r, rbuf), (s, sbuf)))
    ]
    for copy in copies:
        copy.start()
    for copy in copies:
        copy.wait()
    for b in range(height // STRIP):
        at = strip + b - halo // STRIP
        keep = jnp.logical_and(at >= 0, at < u.shape[1] // STRIP)
        here = slice(halo + b * STRIP, halo + (b + 1) * STRIP)
        scale = 1.0 / (1.0 + rbuf[:, here, :])
        parts = ubuf[:, here, :], 0.1 * scale, sbuf[:, here, :] * scale
        put(slice(b * STRIP, (b + 1) * STRIP), [jnp.where(keep, part, 0.0) for part in parts])


def phase(body, intervals=range(PHASE // STEPS)):
    for k in intervals:
        def pair(p, _):
            for n in range(2):
                body(k, 2 * p + n, n)
            return 0
        lax.fori_loop(0, STEPS // 2, pair, 0)
        yield k


def first_iteration(m, q, near_out, far_out, taps, ua, ub, odd, edges):
    t_matrix = z_matrix(taps)

    def step(k, at, n):
        def ghosts(t, c):
            up, down = traces(c)
            rows = series_rows(k, at, t)
            near_out[rows, :] = jnp.where(odd, down, up)
            far_out[rows, :] = jnp.where(odd, up, down)
            return None, None

        src, dst = ((ua, ub), (ub, ua))[n]
        advance(src, dst, m, q, ghosts, edges, range(k, WINDOW // 8 - k), t_matrix)

    for _ in phase(step):
        pass


def first_a_kernel(u, r, s, near_out, far_out, start, m, q, last, taps, ubuf, rbuf, sbuf, ua, ub, sems):
    strip, odd, edges = position()

    def put(rows, parts):
        start[:, rows, :], m[:, rows, :], q[:, rows, :] = parts
        ua[:, PAD + rows.start : PAD + rows.stop, :] = parts[0]

    clear_pads((ua, ub), WINDOW)
    load_window(u, r, s, ubuf, rbuf, sbuf, sems, strip, WINDOW, put)
    first_iteration(m, q, near_out, far_out, taps, ua, ub, odd, edges)
    last[...] = ua[:, PAD + HALO : PAD + HALO + STRIP, :]


def join(strip, even_swap, mid, odd_swap, ua):
    odd_strip = lax.rem(strip, 2) == 1

    def put(left, right):
        for at, part in enumerate((left, mid, right)):
            ua[:, PAD + at * STRIP : PAD + (at + 1) * STRIP, :] = part[...]

    pl.when(odd_strip)(lambda: put(even_swap, odd_swap))
    pl.when(jnp.logical_not(odd_strip))(lambda: put(odd_swap, even_swap))


def first_b_kernel(m, q, even_swap, mid, odd_swap, near_out, far_out, taps, ua, ub):
    strip, odd, edges = position()
    clear_pads((ua, ub), WINDOW)
    join(strip, even_swap, mid, odd_swap, ua)
    first_iteration(m, q, near_out, far_out, taps, ua, ub, odd, edges)


def second_iteration(m, q, near, far, ends, taps, ua, ub, odd, edges):
    t_matrix = z_matrix(taps)

    def step(k, at, n):
        def ghosts(t, c):
            rows = series_rows(k, at, t)
            near_trace, far_trace = near[rows, :], far[rows, :]
            return jnp.where(odd, near_trace, far_trace), jnp.where(odd, far_trace, near_trace)

        src, dst = ((ua, ub), (ub, ua))[n]
        advance(src, dst, m, q, ghosts, edges, range(k, WINDOW // 8 - k), t_matrix)

    for k in phase(step):
        ends[k] = ua[:, PAD + HALO : PAD + HALO + STRIP, :]


def second_a_kernel(start, m, q, near, far, ends, taps, ua, ub):
    _, odd, edges = position()
    clear_pads((ua, ub), WINDOW)
    ua[:, PAD : PAD + WINDOW, :] = start[...]
    second_iteration(m, q, near, far, ends, taps, ua, ub, odd, edges)


def second_b_kernel(m, q, near, far, even_swap, mid, odd_swap, ends, taps, ua, ub):
    strip, odd, edges = position()
    clear_pads((ua, ub), WINDOW)
    join(strip, even_swap, mid, odd_swap, ua)
    second_iteration(m, q, near, far, ends, taps, ua, ub, odd, edges)


def far_partners(slabs):
    for low in range(1, slabs - 1, 2):
        flip = 4 if low + 1 == slabs // 2 else 0
        for at in range(8):
            yield low * 8 + at, (low + 1) * 8 + (at ^ flip)


def swaps(some, others):
    pairs = list(zip(some, others))
    return pairs + [(b, a) for a, b in pairs]


def buffer(rows):
    return pltpu.VMEM((CX, rows, NZ), jnp.float32)


def local(u, r, s):
    slabs = lax.axis_size("gx")
    taps = pltpu.VMEM((2 * NZ, NZ), jnp.bfloat16)
    padded = buffer(WINDOW + 2 * PAD)

    def out(*shape):
        return pltpu.VMEM(shape, jnp.float32)

    def kernel(body, outs, ins, scratch, name, micros, after=0):
        def run(*refs):
            body(*refs[: len(ins)], *refs[len(ins) + after :])

        return pl.pallas_call(
            run,
            out_shape=outs,
            in_specs=ins + [ANY] * after,
            out_specs=jax.tree.map(lambda _: VMEM, outs),
            scratch_shapes=scratch,
            compiler_params=pltpu.CompilerParams(vmem_limit_bytes=16 << 20),
            cost_estimate=pl.CostEstimate(flops=0, transcendentals=0, bytes_accessed=int(micros * 3.6e6)),
            name=name,
        )

    far_pairs = swaps(*zip(*far_partners(slabs)))
    near_pairs = swaps(range(0, slabs, 2), range(1, slabs, 2))
    even_pairs = swaps(SNAKE[0::2], SNAKE[1::2])
    odd_pairs = swaps(SNAKE[1:-1:2], SNAKE[2::2])
    series = out(SERIES, NZ)
    window = out(CX, WINDOW, NZ)
    work = [taps] + [padded] * 2

    def send(near, far):
        return lax.ppermute(near, "gx", near_pairs), lax.ppermute(far, ("gx", "ta"), far_pairs)

    def halo(strip):
        return lax.ppermute(strip, "ta", even_pairs), strip, lax.ppermute(strip, "ta", odd_pairs)

    u, r, s = (pltpu.with_memory_space_constraint(a, pltpu.HBM) for a in (u, r, s))
    near_a, far_a, start, m, q, last = kernel(
        first_a_kernel, (series, series, window, window, window, out(CX, STRIP, NZ)), [HBM] * 3,
        [taps] + [buffer(WINDOW + 2 * HALO)] * 3 + [padded] * 2 + [pltpu.SemaphoreType.DMA((3,))], "first_iteration_a", 6.0,
    )(u, r, s)
    theirs_a = send(near_a, far_a)
    near_b, far_b = kernel(
        first_b_kernel, (series, series), [VMEM] * 5, work, "first_iteration_b", 3.0, 2
    )(m, q, *halo(last), near_a, far_a)
    theirs_b = send(near_b, far_b)
    ends_a = kernel(
        second_a_kernel, out(4, CX, STRIP, NZ), [VMEM] * 5, work, "second_iteration_a", 12.0, 2
    )(start, m, q, *theirs_a, near_b, far_b)
    ends_b = kernel(
        second_b_kernel, out(4, CX, STRIP, NZ), [VMEM] * 7, work, "second_iteration_b", 3.0
    )(m, q, *theirs_b, *halo(ends_a[3]))
    ends = jnp.concatenate([ends_a, ends_b], 0)
    strips = lax.all_to_all(ends, "ta", 0, 0, tiled=True)
    lower = lax.axis_index("gx") < slabs // 2
    return jnp.concatenate([jnp.where(lower, strips[i], strips[i ^ 4]) for i in SNAKE], 1)[None]


def solution(mesh):
    return jax.shard_map(
        local,
        mesh=mesh,
        in_specs=(P("gx", None, None), P("gx", None, None), P("gx", None, None)),
        out_specs=P("ta", "gx", None, None),
        check_vma=False,
    )
```

```python
import jax
import jax.numpy as jnp
from jax import lax
from jax.experimental import pallas as pl
from jax.experimental.pallas import tpu as pltpu
from jax.sharding import PartitionSpec as P

CX = 8
NZ = 128
STRIP = 32
HALO = 32
WINDOW = STRIP + 2 * HALO
PHASE = 32
STEPS = 8
PAD = 8
SERIES = STEPS * sum(range(WINDOW, STRIP, -16))
GROUP = 4
SNAKE = (0, 1, 2, 3, 7, 6, 5, 4)
BY_MATRIX = 4

VMEM = pl.BlockSpec(memory_space=pltpu.VMEM)
ANY = pl.BlockSpec(memory_space=pl.ANY)
HBM = pl.BlockSpec(memory_space=pltpu.HBM)


def z_matrix(taps):
    row = lax.broadcasted_iota(jnp.int32, (NZ, NZ), 0)
    col = lax.broadcasted_iota(jnp.int32, (NZ, NZ), 1)
    half = jnp.where(row == col - 1, 2.0, 0.0) + jnp.where(row == col + 1, 1.0, 0.0)
    taps[:NZ, :] = half.astype(jnp.bfloat16)
    taps[NZ:, :] = half.astype(jnp.bfloat16)
    return taps[...]


def position():
    interval = lax.axis_index("ta")
    slab = lax.axis_index("gx")
    slabs = lax.axis_size("gx")
    strip = jnp.where(interval < 4, interval, 11 - interval)
    strip = jnp.where(slab < slabs // 2, strip, 7 - strip)
    edges = jnp.where(slab > 0, 0.6, 0.0), jnp.where(slab < slabs - 1, 0.6, 0.0)
    return strip, lax.rem(slab, 2) == 1, edges


def z_sum(planes, taps):
    high = planes.astype(jnp.bfloat16)
    low = (planes - high.astype(jnp.float32)).astype(jnp.bfloat16)
    return jnp.dot(jnp.concatenate([high, low], 1), taps, preferred_element_type=jnp.float32)


def advance(src, dst, m, q, ghosts, edge, tiles, taps):
    lane = lax.broadcasted_iota(jnp.int32, (8, NZ), 1)
    not_first, not_last = lane != 0, lane != NZ - 1
    tiles = list(tiles)
    for begin in range(0, len(tiles), GROUP):
        group = tiles[begin : begin + GROUP]
        cells = [[src[x, PAD + 8 * t : PAD + 8 * t + 8, :] for x in range(CX)] for t in group]
        z_all = z_sum(jnp.concatenate([c[x] for c in cells for x in range(BY_MATRIX)], 0), taps)
        for at, t in enumerate(group):
            c = cells[at]
            low, high = ghosts(t, c)
            low = edge[0] * c[0] if low is None else edge[0] * c[0] + low
            high = edge[1] * c[-1] if high is None else edge[1] * c[-1] + high
            below = [low] + c[:-1]
            above = c[1:] + [high]
            for x in range(CX):
                y_below = src[x, PAD + 8 * t - 1 : PAD + 8 * t + 7, :]
                y_above = src[x, PAD + 8 * t + 1 : PAD + 8 * t + 9, :]
                if x < BY_MATRIX:
                    row = (at * BY_MATRIX + x) * 8
                    twice = below[x] + y_below
                    total = (twice + twice) + ((below[x] + above[x]) + y_above) + z_all[row : row + 8]
                else:
                    z_below = jnp.where(not_first, pltpu.roll(c[x], 1, 1), 0.0)
                    z_above = jnp.where(not_last, pltpu.roll(c[x], NZ - 1, 1), 0.0)
                    twice = below[x] + y_below + z_below
                    total = (twice + twice) + ((below[x] + above[x]) + (y_above + z_above))
                rows = slice(8 * t, 8 * t + 8)
                dst[x, PAD + 8 * t : PAD + 8 * t + 8, :] = total * m[x, rows, :] + q[x, rows, :]


def clear_pads(buffers, rows):
    for b in buffers:
        b[:, :PAD, :] = jnp.zeros((CX, PAD, NZ), jnp.float32)
        b[:, PAD + rows :, :] = jnp.zeros((CX, PAD, NZ), jnp.float32)


def traces(c):
    return c[CX - 2] - 0.6 * c[CX - 1], c[1] - 0.6 * c[0]


def series_rows(k, step, t):
    base = STEPS * sum(WINDOW - 16 * before for before in range(k))
    return pl.ds(pl.multiple_of(base + step * (WINDOW - 16 * k) + 8 * (t - k), 8), 8)


def load_window(u, r, s, ubuf, rbuf, sbuf, sems, strip, height, put):
    halo = (height - STRIP) // 2
    first = strip * STRIP - halo
    start = pl.multiple_of(jnp.clip(first, 0, u.shape[1] - height), STRIP)
    landing = pl.multiple_of(halo + start - first, STRIP)
    copies = [
        pltpu.make_async_copy(a.at[:, pl.ds(start, height), :], v.at[:, pl.ds(landing, height), :], sems.at[n])
        for n, (a, v) in enumerate(((u, ubuf), (r, rbuf), (s, sbuf)))
    ]
    for copy in copies:
        copy.start()
    for copy in copies:
        copy.wait()
    for b in range(height // STRIP):
        at = strip + b - halo // STRIP
        keep = jnp.logical_and(at >= 0, at < u.shape[1] // STRIP)
        here = slice(halo + b * STRIP, halo + (b + 1) * STRIP)
        scale = 1.0 / (1.0 + rbuf[:, here, :])
        parts = ubuf[:, here, :], 0.1 * scale, sbuf[:, here, :] * scale
        put(slice(b * STRIP, (b + 1) * STRIP), [jnp.where(keep, part, 0.0) for part in parts])


def phase(body, intervals=range(PHASE // STEPS)):
    for k in intervals:
        def pair(p, _):
            for n in range(2):
                body(k, 2 * p + n, n)
            return 0
        lax.fori_loop(0, STEPS // 2, pair, 0)
        yield k


def first_iteration(m, q, near_out, far_out, taps, ua, ub, odd, edges):
    t_matrix = z_matrix(taps)

    def step(k, at, n):
        def ghosts(t, c):
            up, down = traces(c)
            rows = series_rows(k, at, t)
            near_out[rows, :] = jnp.where(odd, down, up)
            far_out[rows, :] = jnp.where(odd, up, down)
            return None, None

        src, dst = ((ua, ub), (ub, ua))[n]
        advance(src, dst, m, q, ghosts, edges, range(k, WINDOW // 8 - k), t_matrix)

    for _ in phase(step):
        pass


def first_a_kernel(u, r, s, near_out, far_out, start, m, q, last, taps, ubuf, rbuf, sbuf, ua, ub, sems):
    strip, odd, edges = position()

    def put(rows, parts):
        start[:, rows, :], m[:, rows, :], q[:, rows, :] = parts
        ua[:, PAD + rows.start : PAD + rows.stop, :] = parts[0]

    clear_pads((ua, ub), WINDOW)
    load_window(u, r, s, ubuf, rbuf, sbuf, sems, strip, WINDOW, put)
    first_iteration(m, q, near_out, far_out, taps, ua, ub, odd, edges)
    last[...] = ua[:, PAD + HALO : PAD + HALO + STRIP, :]


def join(strip, even_swap, mid, odd_swap, ua):
    odd_strip = lax.rem(strip, 2) == 1

    def put(left, right):
        for at, part in enumerate((left, mid, right)):
            ua[:, PAD + at * STRIP : PAD + (at + 1) * STRIP, :] = part[...]

    pl.when(odd_strip)(lambda: put(even_swap, odd_swap))
    pl.when(jnp.logical_not(odd_strip))(lambda: put(odd_swap, even_swap))


def first_b_kernel(m, q, even_swap, mid, odd_swap, near_out, far_out, taps, ua, ub):
    strip, odd, edges = position()
    clear_pads((ua, ub), WINDOW)
    join(strip, even_swap, mid, odd_swap, ua)
    first_iteration(m, q, near_out, far_out, taps, ua, ub, odd, edges)


def second_iteration(m, q, near, far, ends, taps, ua, ub, odd, edges, places=range(4)):
    t_matrix = z_matrix(taps)

    def step(k, at, n):
        def ghosts(t, c):
            rows = series_rows(k, at, t)
            near_trace, far_trace = near[rows, :], far[rows, :]
            return jnp.where(odd, near_trace, far_trace), jnp.where(odd, far_trace, near_trace)

        src, dst = ((ua, ub), (ub, ua))[n]
        advance(src, dst, m, q, ghosts, edges, range(k, WINDOW // 8 - k), t_matrix)

    for k in phase(step):
        ends[places[k]] = ua[:, PAD + HALO : PAD + HALO + STRIP, :]


def second_a_kernel(start, m, q, near, far, ends, taps, ua, ub):
    _, odd, edges = position()
    clear_pads((ua, ub), WINDOW)
    ua[:, PAD : PAD + WINDOW, :] = start[...]
    second_iteration(m, q, near, far, ends, taps, ua, ub, odd, edges)


def second_b_kernel(m, q, near, far, even_swap, mid, odd_swap, before, blocks, taps, ua, ub):
    strip, odd, edges = position()
    lower = lax.axis_index("gx") < lax.axis_size("gx") // 2
    clear_pads((ua, ub), WINDOW)
    join(strip, even_swap, mid, odd_swap, ua)
    for k in range(4):
        blocks[jnp.where(lower, k, 7 - k)] = before[k]
    places = [jnp.where(lower, 7 - k, k) for k in range(4)]
    second_iteration(m, q, near, far, blocks, taps, ua, ub, odd, edges, places)


def far_partners(slabs):
    for low in range(1, slabs - 1, 2):
        flip = 4 if low + 1 == slabs // 2 else 0
        for at in range(8):
            yield low * 8 + at, (low + 1) * 8 + (at ^ flip)


def swaps(some, others):
    pairs = list(zip(some, others))
    return pairs + [(b, a) for a, b in pairs]


def buffer(rows):
    return pltpu.VMEM((CX, rows, NZ), jnp.float32)


def local(u, r, s):
    slabs = lax.axis_size("gx")
    taps = pltpu.VMEM((2 * NZ, NZ), jnp.bfloat16)
    padded = buffer(WINDOW + 2 * PAD)

    def out(*shape):
        return pltpu.VMEM(shape, jnp.float32)

    def kernel(body, outs, ins, scratch, name, micros, after=0):
        def run(*refs):
            body(*refs[: len(ins)], *refs[len(ins) + after :])

        return pl.pallas_call(
            run,
            out_shape=outs,
            in_specs=ins + [ANY] * after,
            out_specs=jax.tree.map(lambda _: VMEM, outs),
            scratch_shapes=scratch,
            compiler_params=pltpu.CompilerParams(vmem_limit_bytes=16 << 20),
            cost_estimate=pl.CostEstimate(flops=0, transcendentals=0, bytes_accessed=int(micros * 3.6e6)),
            name=name,
        )

    far_pairs = swaps(*zip(*far_partners(slabs)))
    near_pairs = swaps(range(0, slabs, 2), range(1, slabs, 2))
    even_pairs = swaps(SNAKE[0::2], SNAKE[1::2])
    odd_pairs = swaps(SNAKE[1:-1:2], SNAKE[2::2])
    series = out(SERIES, NZ)
    window = out(CX, WINDOW, NZ)
    work = [taps] + [padded] * 2

    def send(near, far):
        return lax.ppermute(near, "gx", near_pairs), lax.ppermute(far, ("gx", "ta"), far_pairs)

    def halo(strip):
        return lax.ppermute(strip, "ta", even_pairs), strip, lax.ppermute(strip, "ta", odd_pairs)

    u, r, s = (pltpu.with_memory_space_constraint(a, pltpu.HBM) for a in (u, r, s))
    near_a, far_a, start, m, q, last = kernel(
        first_a_kernel, (series, series, window, window, window, out(CX, STRIP, NZ)), [HBM] * 3,
        [taps] + [buffer(WINDOW + 2 * HALO)] * 3 + [padded] * 2 + [pltpu.SemaphoreType.DMA((3,))], "first_iteration_a", 6.0,
    )(u, r, s)
    theirs_a = send(near_a, far_a)
    near_b, far_b = kernel(
        first_b_kernel, (series, series), [VMEM] * 5, work, "first_iteration_b", 3.0, 2
    )(m, q, *halo(last), near_a, far_a)
    theirs_b = send(near_b, far_b)
    ends_a = kernel(
        second_a_kernel, out(4, CX, STRIP, NZ), [VMEM] * 5, work, "second_iteration_a", 12.0, 2
    )(start, m, q, *theirs_a, near_b, far_b)
    blocks = kernel(
        second_b_kernel, out(8, CX, STRIP, NZ), [VMEM] * 8, work, "second_iteration_b", 3.0
    )(m, q, *theirs_b, *halo(ends_a[3]), ends_a)
    groups = [[8 * g + (c if g < slabs // 2 else c ^ 4) for c in SNAKE] for g in range(slabs)]
    strips = lax.all_to_all(blocks, ("gx", "ta"), 0, 0, axis_index_groups=groups, tiled=True)
    return strips.transpose(1, 0, 2, 3).reshape(1, CX, -1, NZ)


def solution(mesh):
    return jax.shard_map(
        local,
        mesh=mesh,
        in_specs=(P("gx", None, None), P("gx", None, None), P("gx", None, None)),
        out_specs=P("ta", "gx", None, None),
        check_vma=False,
    )
```

```python
import jax
import jax.numpy as jnp
from jax import lax
from jax.experimental import pallas as pl
from jax.experimental.pallas import tpu as pltpu
from jax.sharding import PartitionSpec as P

CX = 8
NZ = 128
STRIP = 32
HALO = 32
WINDOW = STRIP + 2 * HALO
PHASE = 32
STEPS = 8
PAD = 8
SERIES = STEPS * sum(range(WINDOW, STRIP, -16))
GROUP = 4
SNAKE = (0, 1, 2, 3, 7, 6, 5, 4)
BY_MATRIX = 4

VMEM = pl.BlockSpec(memory_space=pltpu.VMEM)
ANY = pl.BlockSpec(memory_space=pl.ANY)
HBM = pl.BlockSpec(memory_space=pltpu.HBM)


def z_matrix(taps):
    row = lax.broadcasted_iota(jnp.int32, (NZ, NZ), 0)
    col = lax.broadcasted_iota(jnp.int32, (NZ, NZ), 1)
    half = jnp.where(row == col - 1, 2.0, 0.0) + jnp.where(row == col + 1, 1.0, 0.0)
    taps[:NZ, :] = half.astype(jnp.bfloat16)
    taps[NZ:, :] = half.astype(jnp.bfloat16)
    return taps[...]


def position():
    interval = lax.axis_index("ta")
    slab = lax.axis_index("gx")
    slabs = lax.axis_size("gx")
    strip = jnp.where(interval < 4, interval, 11 - interval)
    strip = jnp.where(slab < slabs // 2, strip, 7 - strip)
    edges = jnp.where(slab > 0, 0.6, 0.0), jnp.where(slab < slabs - 1, 0.6, 0.0)
    return strip, lax.rem(slab, 2) == 1, edges


def z_sum(planes, taps):
    high = planes.astype(jnp.bfloat16)
    low = (planes - high.astype(jnp.float32)).astype(jnp.bfloat16)
    return jnp.dot(jnp.concatenate([high, low], 1), taps, preferred_element_type=jnp.float32)


def advance(src, dst, m, q, ghosts, edge, tiles, taps):
    lane = lax.broadcasted_iota(jnp.int32, (8, NZ), 1)
    not_first, not_last = lane != 0, lane != NZ - 1
    tiles = list(tiles)
    for begin in range(0, len(tiles), GROUP):
        group = tiles[begin : begin + GROUP]
        cells = [[src[x, PAD + 8 * t : PAD + 8 * t + 8, :] for x in range(CX)] for t in group]
        z_all = z_sum(jnp.concatenate([c[x] for c in cells for x in range(BY_MATRIX)], 0), taps)
        for at, t in enumerate(group):
            c = cells[at]
            low, high = ghosts(t, c)
            low = edge[0] * c[0] if low is None else edge[0] * c[0] + low
            high = edge[1] * c[-1] if high is None else edge[1] * c[-1] + high
            below = [low] + c[:-1]
            above = c[1:] + [high]
            for x in range(CX):
                y_below = src[x, PAD + 8 * t - 1 : PAD + 8 * t + 7, :]
                y_above = src[x, PAD + 8 * t + 1 : PAD + 8 * t + 9, :]
                if x < BY_MATRIX:
                    row = (at * BY_MATRIX + x) * 8
                    twice = below[x] + y_below
                    total = (twice + twice) + ((below[x] + above[x]) + y_above) + z_all[row : row + 8]
                else:
                    z_below = jnp.where(not_first, pltpu.roll(c[x], 1, 1), 0.0)
                    z_above = jnp.where(not_last, pltpu.roll(c[x], NZ - 1, 1), 0.0)
                    twice = below[x] + y_below + z_below
                    total = (twice + twice) + ((below[x] + above[x]) + (y_above + z_above))
                rows = slice(8 * t, 8 * t + 8)
                dst[x, PAD + 8 * t : PAD + 8 * t + 8, :] = total * m[x, rows, :] + q[x, rows, :]


def clear_pads(buffers, rows):
    for b in buffers:
        b[:, :PAD, :] = jnp.zeros((CX, PAD, NZ), jnp.float32)
        b[:, PAD + rows :, :] = jnp.zeros((CX, PAD, NZ), jnp.float32)


def traces(c):
    return c[CX - 2] - 0.6 * c[CX - 1], c[1] - 0.6 * c[0]


def series_rows(k, step, t):
    base = STEPS * sum(WINDOW - 16 * before for before in range(k))
    return pl.ds(pl.multiple_of(base + step * (WINDOW - 16 * k) + 8 * (t - k), 8), 8)


def load_window(u, r, s, ubuf, rbuf, sbuf, sems, strip, height, put):
    halo = (height - STRIP) // 2
    first = strip * STRIP - halo
    start = pl.multiple_of(jnp.clip(first, 0, u.shape[1] - height), STRIP)
    landing = pl.multiple_of(halo + start - first, STRIP)
    copies = [
        pltpu.make_async_copy(a.at[:, pl.ds(start, height), :], v.at[:, pl.ds(landing, height), :], sems.at[n])
        for n, (a, v) in enumerate(((u, ubuf), (r, rbuf), (s, sbuf)))
    ]
    for copy in copies:
        copy.start()
    for copy in copies:
        copy.wait()
    for b in range(height // STRIP):
        at = strip + b - halo // STRIP
        keep = jnp.logical_and(at >= 0, at < u.shape[1] // STRIP)
        here = slice(halo + b * STRIP, halo + (b + 1) * STRIP)
        scale = 1.0 / (1.0 + rbuf[:, here, :])
        parts = ubuf[:, here, :], 0.1 * scale, sbuf[:, here, :] * scale
        put(slice(b * STRIP, (b + 1) * STRIP), [jnp.where(keep, part, 0.0) for part in parts])


def phase(body, intervals=range(PHASE // STEPS)):
    for k in intervals:
        def pair(p, _):
            for n in range(2):
                body(k, 2 * p + n, n)
            return 0
        lax.fori_loop(0, STEPS // 2, pair, 0)
        yield k


def first_iteration(m, q, near_out, far_out, taps, ua, ub, odd, edges):
    t_matrix = z_matrix(taps)

    def step(k, at, n):
        def ghosts(t, c):
            up, down = traces(c)
            rows = series_rows(k, at, t)
            near_out[rows, :] = jnp.where(odd, down, up)
            far_out[rows, :] = jnp.where(odd, up, down)
            return None, None

        src, dst = ((ua, ub), (ub, ua))[n]
        advance(src, dst, m, q, ghosts, edges, range(k, WINDOW // 8 - k), t_matrix)

    for _ in phase(step):
        pass


def first_a_kernel(u, r, s, near_out, far_out, start, m, q, last, taps, ubuf, rbuf, sbuf, ua, ub, sems):
    strip, odd, edges = position()

    def put(rows, parts):
        start[:, rows, :], m[:, rows, :], q[:, rows, :] = parts
        ua[:, PAD + rows.start : PAD + rows.stop, :] = parts[0]

    clear_pads((ua, ub), WINDOW)
    load_window(u, r, s, ubuf, rbuf, sbuf, sems, strip, WINDOW, put)
    first_iteration(m, q, near_out, far_out, taps, ua, ub, odd, edges)
    last[...] = ua[:, PAD + HALO : PAD + HALO + STRIP, :]


def join(strip, even_swap, mid, odd_swap, ua):
    odd_strip = lax.rem(strip, 2) == 1

    def put(left, right):
        for at, part in enumerate((left, mid, right)):
            ua[:, PAD + at * STRIP : PAD + (at + 1) * STRIP, :] = part[...]

    pl.when(odd_strip)(lambda: put(even_swap, odd_swap))
    pl.when(jnp.logical_not(odd_strip))(lambda: put(odd_swap, even_swap))


def first_b_kernel(m, q, even_swap, mid, odd_swap, near_out, far_out, taps, ua, ub):
    strip, odd, edges = position()
    clear_pads((ua, ub), WINDOW)
    join(strip, even_swap, mid, odd_swap, ua)
    first_iteration(m, q, near_out, far_out, taps, ua, ub, odd, edges)


def second_iteration(m, q, near, far, ends, taps, ua, ub, odd, edges, places=range(4)):
    t_matrix = z_matrix(taps)

    def step(k, at, n):
        def ghosts(t, c):
            rows = series_rows(k, at, t)
            near_trace, far_trace = near[rows, :], far[rows, :]
            return jnp.where(odd, near_trace, far_trace), jnp.where(odd, far_trace, near_trace)

        src, dst = ((ua, ub), (ub, ua))[n]
        advance(src, dst, m, q, ghosts, edges, range(k, WINDOW // 8 - k), t_matrix)

    for k in phase(step):
        ends[places[k]] = ua[:, PAD + HALO : PAD + HALO + STRIP, :]


def second_a_kernel(start, m, q, near, far, ends, taps, ua, ub):
    _, odd, edges = position()
    clear_pads((ua, ub), WINDOW)
    ua[:, PAD : PAD + WINDOW, :] = start[...]
    second_iteration(m, q, near, far, ends, taps, ua, ub, odd, edges)


def second_b_kernel(m, q, near, far, even_swap, mid, odd_swap, before, blocks, taps, ua, ub):
    strip, odd, edges = position()
    lower = lax.axis_index("gx") < lax.axis_size("gx") // 2
    clear_pads((ua, ub), WINDOW)
    join(strip, even_swap, mid, odd_swap, ua)
    for k in range(4):
        blocks[jnp.where(lower, k, 7 - k)] = before[k]
    places = [jnp.where(lower, 7 - k, k) for k in range(4)]
    second_iteration(m, q, near, far, blocks, taps, ua, ub, odd, edges, places)


def far_partners(slabs):
    for low in range(1, slabs - 1, 2):
        flip = 4 if low + 1 == slabs // 2 else 0
        for at in range(8):
            yield low * 8 + at, (low + 1) * 8 + (at ^ flip)


def swaps(some, others):
    pairs = list(zip(some, others))
    return pairs + [(b, a) for a, b in pairs]


def buffer(rows):
    return pltpu.VMEM((CX, rows, NZ), jnp.float32)


def local(u, r, s):
    slabs = lax.axis_size("gx")
    taps = pltpu.VMEM((2 * NZ, NZ), jnp.bfloat16)
    padded = buffer(WINDOW + 2 * PAD)

    def out(*shape):
        return pltpu.VMEM(shape, jnp.float32)

    def kernel(body, outs, ins, scratch, name, micros, after=0):
        def run(*refs):
            body(*refs[: len(ins)], *refs[len(ins) + after :])

        return pl.pallas_call(
            run,
            out_shape=outs,
            in_specs=ins + [ANY] * after,
            out_specs=jax.tree.map(lambda _: VMEM, outs),
            scratch_shapes=scratch,
            compiler_params=pltpu.CompilerParams(vmem_limit_bytes=16 << 20),
            cost_estimate=pl.CostEstimate(flops=0, transcendentals=0, bytes_accessed=int(micros * 3.6e6)),
            name=name,
        )

    far_pairs = swaps(*zip(*far_partners(slabs)))
    near_pairs = swaps(range(0, slabs, 2), range(1, slabs, 2))
    even_pairs = swaps(SNAKE[0::2], SNAKE[1::2])
    odd_pairs = swaps(SNAKE[1:-1:2], SNAKE[2::2])
    series = out(SERIES, NZ)
    window = out(CX, WINDOW, NZ)
    work = [taps] + [padded] * 2

    def send(near, far):
        return lax.ppermute(near, "gx", near_pairs), lax.ppermute(far, ("gx", "ta"), far_pairs)

    def halo(strip):
        return lax.ppermute(strip, "ta", even_pairs), strip, lax.ppermute(strip, "ta", odd_pairs)

    u, r, s = (pltpu.with_memory_space_constraint(a, pltpu.HBM) for a in (u, r, s))
    near_a, far_a, start, m, q, last = kernel(
        first_a_kernel, (series, series, window, window, window, out(CX, STRIP, NZ)), [HBM] * 3,
        [taps] + [buffer(WINDOW + 2 * HALO)] * 3 + [padded] * 2 + [pltpu.SemaphoreType.DMA((3,))], "first_iteration_a", 6.0,
    )(u, r, s)
    far_a_in = lax.ppermute(far_a, ("gx", "ta"), far_pairs)
    near_b, far_b = kernel(
        first_b_kernel, (series, series), [VMEM] * 5, work, "first_iteration_b", 3.0, 2
    )(m, q, *halo(last), near_a, far_a)
    near_a, near_b, far_b = lax.optimization_barrier((near_a, near_b, far_b))
    theirs_a = lax.ppermute(near_a, "gx", near_pairs), far_a_in
    theirs_b = send(near_b, far_b)
    ends_a = kernel(
        second_a_kernel, out(4, CX, STRIP, NZ), [VMEM] * 5, work, "second_iteration_a", 12.0, 2
    )(start, m, q, *theirs_a, near_b, far_b)
    blocks = kernel(
        second_b_kernel, out(8, CX, STRIP, NZ), [VMEM] * 8, work, "second_iteration_b", 3.0
    )(m, q, *theirs_b, *halo(ends_a[3]), ends_a)
    groups = [[8 * g + (c if g < slabs // 2 else c ^ 4) for c in SNAKE] for g in range(slabs)]
    strips = lax.all_to_all(blocks, ("gx", "ta"), 0, 0, axis_index_groups=groups, tiled=True)
    return strips.transpose(1, 0, 2, 3).reshape(1, CX, -1, NZ)


def solution(mesh):
    return jax.shard_map(
        local,
        mesh=mesh,
        in_specs=(P("gx", None, None), P("gx", None, None), P("gx", None, None)),
        out_specs=P("ta", "gx", None, None),
        check_vma=False,
    )
```

```python
import jax
import jax.numpy as jnp
from jax import lax
from jax.experimental import pallas as pl
from jax.experimental.pallas import tpu as pltpu
from jax.sharding import PartitionSpec as P

CX = 8
NZ = 128
STRIP = 32
HALO = 32
WINDOW = STRIP + 2 * HALO
PHASE = 32
STEPS = 8
PAD = 8
SERIES = STEPS * sum(range(WINDOW, STRIP, -16))
GROUP = 6
SNAKE = (0, 1, 2, 3, 7, 6, 5, 4)
BY_MATRIX = 4

VMEM = pl.BlockSpec(memory_space=pltpu.VMEM)
ANY = pl.BlockSpec(memory_space=pl.ANY)
HBM = pl.BlockSpec(memory_space=pltpu.HBM)


def z_matrix(taps):
    row = lax.broadcasted_iota(jnp.int32, (NZ, NZ), 0)
    col = lax.broadcasted_iota(jnp.int32, (NZ, NZ), 1)
    half = jnp.where(row == col - 1, 2.0, 0.0) + jnp.where(row == col + 1, 1.0, 0.0)
    taps[:NZ, :] = half.astype(jnp.bfloat16)
    taps[NZ:, :] = half.astype(jnp.bfloat16)
    return taps[...]


def position():
    interval = lax.axis_index("ta")
    slab = lax.axis_index("gx")
    slabs = lax.axis_size("gx")
    strip = jnp.where(interval < 4, interval, 11 - interval)
    strip = jnp.where(slab < slabs // 2, strip, 7 - strip)
    edges = jnp.where(slab > 0, 0.6, 0.0), jnp.where(slab < slabs - 1, 0.6, 0.0)
    return strip, lax.rem(slab, 2) == 1, edges


def z_sum(planes, taps):
    high = planes.astype(jnp.bfloat16)
    low = (planes - high.astype(jnp.float32)).astype(jnp.bfloat16)
    return jnp.dot(jnp.concatenate([high, low], 1), taps, preferred_element_type=jnp.float32)


def advance(src, dst, m, q, ghosts, edge, tiles, taps):
    lane = lax.broadcasted_iota(jnp.int32, (8, NZ), 1)
    not_first, not_last = lane != 0, lane != NZ - 1
    tiles = list(tiles)
    groups = -(-len(tiles) // GROUP)
    for n in range(groups):
        group = tiles[n * len(tiles) // groups : (n + 1) * len(tiles) // groups]
        cells = [[src[x, PAD + 8 * t : PAD + 8 * t + 8, :] for x in range(CX)] for t in group]
        z_all = z_sum(jnp.concatenate([c[x] for c in cells for x in range(BY_MATRIX)], 0), taps)
        for at, t in enumerate(group):
            c = cells[at]
            low, high = ghosts(t, c)
            low = edge[0] * c[0] if low is None else edge[0] * c[0] + low
            high = edge[1] * c[-1] if high is None else edge[1] * c[-1] + high
            below = [low] + c[:-1]
            above = c[1:] + [high]
            for x in range(CX):
                y_below = src[x, PAD + 8 * t - 1 : PAD + 8 * t + 7, :]
                y_above = src[x, PAD + 8 * t + 1 : PAD + 8 * t + 9, :]
                if x < BY_MATRIX:
                    row = (at * BY_MATRIX + x) * 8
                    twice = below[x] + y_below
                    total = (twice + twice) + ((below[x] + above[x]) + y_above) + z_all[row : row + 8]
                else:
                    z_below = jnp.where(not_first, pltpu.roll(c[x], 1, 1), 0.0)
                    z_above = jnp.where(not_last, pltpu.roll(c[x], NZ - 1, 1), 0.0)
                    twice = below[x] + y_below + z_below
                    total = (twice + twice) + ((below[x] + above[x]) + (y_above + z_above))
                rows = slice(8 * t, 8 * t + 8)
                dst[x, PAD + 8 * t : PAD + 8 * t + 8, :] = total * m[x, rows, :] + q[x, rows, :]


def clear_pads(buffers, rows):
    for b in buffers:
        b[:, :PAD, :] = jnp.zeros((CX, PAD, NZ), jnp.float32)
        b[:, PAD + rows :, :] = jnp.zeros((CX, PAD, NZ), jnp.float32)


def traces(c):
    return c[CX - 2] - 0.6 * c[CX - 1], c[1] - 0.6 * c[0]


def series_rows(k, step, t):
    base = STEPS * sum(WINDOW - 16 * before for before in range(k))
    return pl.ds(pl.multiple_of(base + step * (WINDOW - 16 * k) + 8 * (t - k), 8), 8)


def load_window(u, r, s, ubuf, rbuf, sbuf, sems, strip, height, put):
    halo = (height - STRIP) // 2
    first = strip * STRIP - halo
    start = pl.multiple_of(jnp.clip(first, 0, u.shape[1] - height), STRIP)
    landing = pl.multiple_of(halo + start - first, STRIP)
    copies = [
        pltpu.make_async_copy(a.at[:, pl.ds(start, height), :], v.at[:, pl.ds(landing, height), :], sems.at[n])
        for n, (a, v) in enumerate(((u, ubuf), (r, rbuf), (s, sbuf)))
    ]
    for copy in copies:
        copy.start()
    for copy in copies:
        copy.wait()
    for b in range(height // STRIP):
        at = strip + b - halo // STRIP
        keep = jnp.logical_and(at >= 0, at < u.shape[1] // STRIP)
        here = slice(halo + b * STRIP, halo + (b + 1) * STRIP)
        scale = 1.0 / (1.0 + rbuf[:, here, :])
        parts = ubuf[:, here, :], 0.1 * scale, sbuf[:, here, :] * scale
        put(slice(b * STRIP, (b + 1) * STRIP), [jnp.where(keep, part, 0.0) for part in parts])


def phase(body, intervals=range(PHASE // STEPS)):
    for k in intervals:
        def pair(p, _):
            for n in range(2):
                body(k, 2 * p + n, n)
            return 0
        lax.fori_loop(0, STEPS // 2, pair, 0)
        yield k


def first_iteration(m, q, near_out, far_out, taps, ua, ub, odd, edges):
    t_matrix = z_matrix(taps)

    def step(k, at, n):
        def ghosts(t, c):
            up, down = traces(c)
            rows = series_rows(k, at, t)
            near_out[rows, :] = jnp.where(odd, down, up)
            far_out[rows, :] = jnp.where(odd, up, down)
            return None, None

        src, dst = ((ua, ub), (ub, ua))[n]
        advance(src, dst, m, q, ghosts, edges, range(k, WINDOW // 8 - k), t_matrix)

    for _ in phase(step):
        pass


def first_a_kernel(u, r, s, near_out, far_out, start, m, q, last, taps, ubuf, rbuf, sbuf, ua, ub, sems):
    strip, odd, edges = position()

    def put(rows, parts):
        start[:, rows, :], m[:, rows, :], q[:, rows, :] = parts
        ua[:, PAD + rows.start : PAD + rows.stop, :] = parts[0]

    clear_pads((ua, ub), WINDOW)
    load_window(u, r, s, ubuf, rbuf, sbuf, sems, strip, WINDOW, put)
    first_iteration(m, q, near_out, far_out, taps, ua, ub, odd, edges)
    last[...] = ua[:, PAD + HALO : PAD + HALO + STRIP, :]


def join(strip, even_swap, mid, odd_swap, ua):
    odd_strip = lax.rem(strip, 2) == 1

    def put(left, right):
        for at, part in enumerate((left, mid, right)):
            ua[:, PAD + at * STRIP : PAD + (at + 1) * STRIP, :] = part[...]

    pl.when(odd_strip)(lambda: put(even_swap, odd_swap))
    pl.when(jnp.logical_not(odd_strip))(lambda: put(odd_swap, even_swap))


def first_b_kernel(m, q, even_swap, mid, odd_swap, near_out, far_out, taps, ua, ub):
    strip, odd, edges = position()
    clear_pads((ua, ub), WINDOW)
    join(strip, even_swap, mid, odd_swap, ua)
    first_iteration(m, q, near_out, far_out, taps, ua, ub, odd, edges)


def second_iteration(m, q, near, far, ends, taps, ua, ub, odd, edges, places=range(4)):
    t_matrix = z_matrix(taps)

    def step(k, at, n):
        def ghosts(t, c):
            rows = series_rows(k, at, t)
            near_trace, far_trace = near[rows, :], far[rows, :]
            return jnp.where(odd, near_trace, far_trace), jnp.where(odd, far_trace, near_trace)

        src, dst = ((ua, ub), (ub, ua))[n]
        advance(src, dst, m, q, ghosts, edges, range(k, WINDOW // 8 - k), t_matrix)

    for k in phase(step):
        ends[places[k]] = ua[:, PAD + HALO : PAD + HALO + STRIP, :]


def second_a_kernel(start, m, q, near, far, ends, taps, ua, ub):
    _, odd, edges = position()
    clear_pads((ua, ub), WINDOW)
    ua[:, PAD : PAD + WINDOW, :] = start[...]
    second_iteration(m, q, near, far, ends, taps, ua, ub, odd, edges)


def second_b_kernel(m, q, near, far, even_swap, mid, odd_swap, before, blocks, taps, ua, ub):
    strip, odd, edges = position()
    lower = lax.axis_index("gx") < lax.axis_size("gx") // 2
    clear_pads((ua, ub), WINDOW)
    join(strip, even_swap, mid, odd_swap, ua)
    for k in range(4):
        blocks[jnp.where(lower, k, 7 - k)] = before[k]
    places = [jnp.where(lower, 7 - k, k) for k in range(4)]
    second_iteration(m, q, near, far, blocks, taps, ua, ub, odd, edges, places)


def far_partners(slabs):
    for low in range(1, slabs - 1, 2):
        flip = 4 if low + 1 == slabs // 2 else 0
        for at in range(8):
            yield low * 8 + at, (low + 1) * 8 + (at ^ flip)


def swaps(some, others):
    pairs = list(zip(some, others))
    return pairs + [(b, a) for a, b in pairs]


def buffer(rows):
    return pltpu.VMEM((CX, rows, NZ), jnp.float32)


def local(u, r, s):
    slabs = lax.axis_size("gx")
    taps = pltpu.VMEM((2 * NZ, NZ), jnp.bfloat16)
    padded = buffer(WINDOW + 2 * PAD)

    def out(*shape):
        return pltpu.VMEM(shape, jnp.float32)

    def kernel(body, outs, ins, scratch, name, micros, after=0):
        def run(*refs):
            body(*refs[: len(ins)], *refs[len(ins) + after :])

        return pl.pallas_call(
            run,
            out_shape=outs,
            in_specs=ins + [ANY] * after,
            out_specs=jax.tree.map(lambda _: VMEM, outs),
            scratch_shapes=scratch,
            compiler_params=pltpu.CompilerParams(vmem_limit_bytes=16 << 20),
            cost_estimate=pl.CostEstimate(flops=0, transcendentals=0, bytes_accessed=int(micros * 3.6e6)),
            name=name,
        )

    far_pairs = swaps(*zip(*far_partners(slabs)))
    near_pairs = swaps(range(0, slabs, 2), range(1, slabs, 2))
    even_pairs = swaps(SNAKE[0::2], SNAKE[1::2])
    odd_pairs = swaps(SNAKE[1:-1:2], SNAKE[2::2])
    series = out(SERIES, NZ)
    window = out(CX, WINDOW, NZ)
    work = [taps] + [padded] * 2

    def send(near, far):
        return lax.ppermute(near, "gx", near_pairs), lax.ppermute(far, ("gx", "ta"), far_pairs)

    def halo(strip):
        return lax.ppermute(strip, "ta", even_pairs), strip, lax.ppermute(strip, "ta", odd_pairs)

    u, r, s = (pltpu.with_memory_space_constraint(a, pltpu.HBM) for a in (u, r, s))
    near_a, far_a, start, m, q, last = kernel(
        first_a_kernel, (series, series, window, window, window, out(CX, STRIP, NZ)), [HBM] * 3,
        [taps] + [buffer(WINDOW + 2 * HALO)] * 3 + [padded] * 2 + [pltpu.SemaphoreType.DMA((3,))], "first_iteration_a", 6.0,
    )(u, r, s)
    far_a_in = lax.ppermute(far_a, ("gx", "ta"), far_pairs)
    near_b, far_b = kernel(
        first_b_kernel, (series, series), [VMEM] * 5, work, "first_iteration_b", 3.0, 2
    )(m, q, *halo(last), near_a, far_a)
    near_a, near_b, far_b = lax.optimization_barrier((near_a, near_b, far_b))
    theirs_a = lax.ppermute(near_a, "gx", near_pairs), far_a_in
    theirs_b = send(near_b, far_b)
    ends_a = kernel(
        second_a_kernel, out(4, CX, STRIP, NZ), [VMEM] * 5, work, "second_iteration_a", 12.0, 2
    )(start, m, q, *theirs_a, near_b, far_b)
    blocks = kernel(
        second_b_kernel, out(8, CX, STRIP, NZ), [VMEM] * 8, work, "second_iteration_b", 3.0
    )(m, q, *theirs_b, *halo(ends_a[3]), ends_a)
    groups = [[8 * g + (c if g < slabs // 2 else c ^ 4) for c in SNAKE] for g in range(slabs)]
    strips = lax.all_to_all(blocks, ("gx", "ta"), 0, 0, axis_index_groups=groups, tiled=True)
    return strips.transpose(1, 0, 2, 3).reshape(1, CX, -1, NZ)


def solution(mesh):
    return jax.shard_map(
        local,
        mesh=mesh,
        in_specs=(P("gx", None, None), P("gx", None, None), P("gx", None, None)),
        out_specs=P("ta", "gx", None, None),
        check_vma=False,
    )
```
